32 devices in a mesh: grp: 4 (over x, core), tp: 8 (over z, y).
Axes of the slice: x: 2, y: 2, z: 4, core: 2. Of those that a mesh axis runs over, the one named last changes fastest.
Arguments:
- in_panels: bfloat16 [8, 1024, 2, 8192], P('grp', None, None, 'tp'), may hold values from -0.0625 to 0.0625
- layout: int32 [8], replicated, may hold values from 0 to 7, each once
- hidden: bfloat16 [128, 16, 8192], P('grp', None, 'tp'), may hold values from -6 to 6
- prompt_state: float32 [16, 19, 8192], P('grp', None, 'tp'), may hold values from -6 to 6
- fork_counts: int32 [4, 16], replicated, may hold values from 0 to 16, as said below
- conv_weight: float32 [4, 8192], P(None, 'tp'), may hold values from -0.8 to 0.8
- conv_bias: float32 [8192], P('tp'), may hold values from -0.5 to 0.5
- x_weight: bfloat16 [8192, 544], P('tp'), may hold values from -0.0625 to 0.0625
- dt_weight: bfloat16 [512, 8192], P(None, 'tp'), may hold values from -0.25 to 0.25
- dt_bias: float32 [8192], P('tp'), may hold values from -6 to -2
- decay_rate: float32 [16, 8192], P(None, 'tp'), may hold values from 0.5 to 8
- skip_gain: float32 [8192], P('tp'), may hold values from 0.5 to 1.5
Outputs:
- mixed: bfloat16 [128, 16, 8192], P('grp', None, 'tp')
- final_state: float32 [128, 19, 8192], P('grp', None, 'tp')
The draws below stay inside these ranges and needn't reach their ends.
Inputs may be any that keep to these rules, and one draw needn't show every extreme that they name: `layout`: A permutation of the panel slots. Each row sums to 32: group g's sequences fork the prompts in order, prompt p taking fork_counts[g, p] of them. In every row some prompt takes exactly 16.
All inputs are finite; a program needn't handle non-finite values.
Results may differ from the reference program's by a relative error of at most 0.0069.
Values may be sent and summed in bfloat16 or wider, within the bound.
A program may use at most 192 MiB of HBM per device.

```python
import math
import jax
import jax.numpy as jnp
from jax import lax

D = 8192
DI = 8192
N = 16
R = 512
KC = 4
STEPS = 16
SEQ = 32
GROUPS = 4
NPAN = 8
PR = 1024
NPR = 16
NSEQ = 128


def draw_fork_counts(key, part):
    key = jax.random.fold_in(key, 7)
    busy_key, other_key = jax.random.split(key)
    busy = jax.random.randint(busy_key, (GROUPS, 1), 0, NPR)
    others = jax.random.randint(other_key, (GROUPS, SEQ), 0, NPR - 1)
    others = others + (others >= busy).astype(jnp.int32)
    slot_ids = jnp.arange(SEQ, dtype=jnp.int32)[None, :]
    picks = jnp.where(slot_ids < SEQ // 2, busy, others)
    prompt_ids = jnp.arange(NPR, dtype=jnp.int32)
    return jnp.sum((picks[:, :, None] == prompt_ids[None, None, :]).astype(jnp.int32), axis=1)


def steps_of(own_key, extent, shards, low, high):
    level, own = 1.0, jax.random.fold_in(own_key, 6)
    for position, blocks in shards:
        draws = jnp.exp(jax.random.uniform(jax.random.fold_in(own, position), (blocks,), jnp.float32, low / len(shards), high / len(shards)))
        level = level * jnp.repeat(draws, extent[position] // blocks).reshape([-1 if axis == position else 1 for axis in range(len(extent))])
    return level


def gaussian(stream_key, dims, spread, most, shards=(), kind=jnp.bfloat16):
    array = spread * jax.random.normal(stream_key, dims, jnp.float32)
    if shards:
        array = array * steps_of(stream_key, dims, shards, -0.22, 0.18)
    return jnp.clip(array, -most, most).astype(kind)


def setup_inputs(seed: int = 0) -> dict:
    key_of = jax.random.split(jax.random.key(seed), 13)
    in_panels = gaussian(key_of[0], (NPAN, PR, 2, DI), D ** -0.5, 0.0625, ((0, 4), (3, 8)))
    layout = jax.random.permutation(key_of[1], NPAN).astype(jnp.int32)
    hidden = gaussian(key_of[2], (NSEQ, STEPS, D), 1.0, 6.0, ((0, 4), (2, 8)))
    prompt_state = gaussian(key_of[3], (NPR, KC - 1 + N, DI), 1.0, 6.0, ((0, 4), (2, 8)), jnp.float32)
    fork_counts = draw_fork_counts(jax.random.fold_in(key_of[12], 71), 0)
    conv_weight = jnp.clip(jax.random.uniform(key_of[5], (KC, DI), jnp.float32, -0.8, 0.8) * steps_of(key_of[5], (KC, DI), ((1, 8),), -0.4, 0.0), -0.8, 0.8)
    conv_bias = jnp.clip(jax.random.uniform(key_of[6], (DI,), jnp.float32, -0.5, 0.5) * steps_of(key_of[6], (DI,), ((0, 8),), -0.4, 0.0), -0.5, 0.5)
    x_weight = gaussian(key_of[7], (DI, R + 2 * N), DI ** -0.5, 0.0625, ((0, 8),))
    dt_weight = gaussian(key_of[8], (R, DI), R ** -0.5, 0.25, ((1, 8),))
    dt_bias = jnp.clip(-6.0 + 4.0 * jax.random.uniform(key_of[9], (DI,), jnp.float32) ** steps_of(key_of[9], (DI,), ((0, 8),), -0.2, 0.2), -6.0, -2.0)
    decay_rate = jnp.clip(jnp.exp(math.log(8.0) - 2.7725887 * jax.random.uniform(key_of[10], (N, DI), jnp.float32) ** steps_of(key_of[10], (N, DI), ((1, 8),), -0.2, 0.2)), 0.5, 8.0)
    skip_gain = jnp.clip(0.5 + 1.0 * jax.random.uniform(key_of[11], (DI,), jnp.float32) ** steps_of(key_of[11], (DI,), ((0, 8),), -0.2, 0.2), 0.5, 1.5)
    return {"in_panels": in_panels, "layout": layout, "hidden": hidden, "prompt_state": prompt_state, "fork_counts": fork_counts, "conv_weight": conv_weight, "conv_bias": conv_bias, "x_weight": x_weight, "dt_weight": dt_weight, "dt_bias": dt_bias, "decay_rate": decay_rate, "skip_gain": skip_gain}


def fork_sources(counts, per_group):
    running = jnp.cumsum(counts, axis=1)
    slot_ids = jnp.arange(per_group, dtype=jnp.int32)
    return jnp.sum((running[:, None, :] <= slot_ids[None, :, None]).astype(jnp.int32), axis=2)


def reference(in_panels, layout, hidden, prompt_state, fork_counts, conv_weight, conv_bias, x_weight, dt_weight, dt_bias, decay_rate, skip_gain):
    row_count = NSEQ * STEPS
    blocks = hidden.reshape(row_count, NPAN, PR)
    ordered = jnp.take(blocks, layout.astype(jnp.int32), axis=1).reshape(row_count, D)
    projected = jnp.dot(ordered, in_panels.reshape(D, 2 * DI), preferred_element_type=jnp.float32)
    projected = projected.reshape(NSEQ, STEPS, 2, DI)
    x_in = projected[:, :, 0].astype(jnp.bfloat16)
    gate_z = projected[:, :, 1].astype(jnp.bfloat16)
    sources = fork_sources(fork_counts, SEQ).reshape(-1).astype(jnp.int32)
    start_state = prompt_state[sources]
    window = jnp.concatenate([start_state[:, :KC - 1], x_in.astype(jnp.float32)], axis=1)
    conv_out = conv_bias + sum(conv_weight[tap] * window[:, tap:tap + STEPS] for tap in range(KC))
    xc = jax.nn.silu(conv_out).astype(jnp.bfloat16)
    dbc = jnp.dot(xc.reshape(row_count, DI), x_weight, preferred_element_type=jnp.float32)
    dt_low = dbc[:, :R].astype(jnp.bfloat16)
    b_in = dbc[:, R:R + N].reshape(NSEQ, STEPS, N)
    c_out = dbc[:, R + N:].reshape(NSEQ, STEPS, N)
    step_size = jax.nn.softplus(jnp.dot(dt_low, dt_weight, preferred_element_type=jnp.float32) + dt_bias)
    step_size = step_size.reshape(NSEQ, STEPS, DI)

    def advance(state, inputs):
        step_now, b_now, c_now, xc_now, z_now = inputs
        xc_float = xc_now.astype(jnp.float32)
        decay = jnp.exp(-step_now[:, None, :] * decay_rate[None])
        state = decay * state + step_now[:, None, :] * b_now[:, :, None] * xc_float[:, None, :]
        output = jnp.sum(c_now[:, :, None] * state, axis=1) + skip_gain * xc_float
        output = output * jax.nn.silu(z_now.astype(jnp.float32))
        return state, output.astype(jnp.bfloat16)

    inputs = (jnp.moveaxis(step_size, 1, 0), jnp.moveaxis(b_in, 1, 0), jnp.moveaxis(c_out, 1, 0), jnp.moveaxis(xc, 1, 0), jnp.moveaxis(gate_z, 1, 0))
    state, outputs = lax.scan(advance, start_state[:, KC - 1:], inputs)
    mixed = jnp.moveaxis(outputs, 0, 1)
    final_state = jnp.concatenate([x_in[:, STEPS - (KC - 1):].astype(jnp.float32), state], axis=1)
    return mixed, final_state
```

```python
import functools

import jax
import jax.numpy as jnp
from jax import lax
from jax.experimental import pallas as pl
from jax.experimental.pallas import tpu as pltpu
from jax.sharding import PartitionSpec as P

MESH = pl.DeviceIdType.MESH
MIB = 1024 * 1024


def fork_sources(counts, per_group):
    running = jnp.cumsum(counts, axis=1)
    slot_ids = jnp.arange(per_group, dtype=jnp.int32)
    return jnp.sum((running[:, None, :] <= slot_ids[None, :, None]).astype(jnp.int32), axis=2)


def ring_place(index, size):
    major, minor = index // 2, index % 2
    return jnp.where(minor == 0, major, size - 1 - major)


def ring_index(place, size):
    place = lax.rem(place + 2 * size, size)
    return jnp.where(place < size // 2, 2 * place, 2 * (size - 1 - place) + 1)


def meet(peers):
    barrier = pltpu.get_barrier_semaphore()
    for peer in peers:
        pl.semaphore_signal(barrier, inc=1, device_id=peer, device_id_type=MESH)
    pl.semaphore_wait(barrier, len(peers))


def project_kernel(
    groups, size, layout_ref, hid_ref, w_hbm, out_ref,
    w_ref, blocks, picked, act, send1, recv1, own, fin, recv2,
    w_sem, a_send, a_recv, b_send, b_recv, r_send, r_recv, s1_send, s1_recv, s2_send, s2_recv,
):
    grp, tp = lax.axis_index("grp"), lax.axis_index("tp")
    outers = groups // 2
    outer, core = grp // 2, grp % 2
    partner = outer * 2 + 1 - core
    parts, _, seqs, panel_rows = hid_ref.shape
    depth = 2 * panel_rows
    width = w_ref.shape[1]
    place = ring_place(tp, size)
    right, left = ring_index(place + 1, size), ring_index(place - 1, size)

    def remote(src, dst, send, recv, g, t):
        return pltpu.make_async_remote_copy(
            src_ref=src, dst_ref=dst, send_sem=send, recv_sem=recv,
            device_id=(g, t), device_id_type=MESH,
        )

    load_w = pltpu.make_async_copy(w_hbm, w_ref, w_sem)
    load_w.start()
    meet(
        [(grp, lax.rem(tp + d, size)) for d in range(1, size)]
        + [(lax.rem(grp + d, groups), tp) for d in range(1, groups)]
    )

    spread = []
    for d in range(1, size):
        to = lax.rem(tp + d, size)
        copy = remote(
            hid_ref.at[:, pl.ds(2 * to, 2)], blocks.at[pl.ds(tp * parts, parts)],
            a_send.at[d], a_recv.at[d], grp, to,
        )
        copy.start()
        spread.append(copy)
    blocks[pl.ds(tp * parts, parts)] = hid_ref[:, pl.ds(2 * tp, 2)]
    for copy in spread:
        copy.wait_recv()

    handed = []
    for d in range(1, groups + 1):
        to = lax.rem(grp + d, groups)
        for j in range(2):
            block = blocks[layout_ref[2 * to + j]]
            columns = slice(j * panel_rows, (j + 1) * panel_rows)
            if d < groups:
                picked[d - 1, :, :, columns] = block
            else:
                act[0, :, grp, :, columns] = block
        if d < groups:
            copy = remote(
                picked.at[d - 1], act.at[0, :, grp], b_send.at[d], b_recv.at[d], to, tp
            )
            copy.start()
            handed.append(copy)
    load_w.wait()
    for copy in handed:
        copy.wait_recv()

    def ring(step, way):
        return remote(
            act.at[step, way], act.at[step + 1, way],
            r_send.at[step, way], r_recv.at[step, way], grp, (right, left)[way],
        )

    def swap(step):
        return remote(
            send1, recv1.at[step], s1_send.at[step], s1_recv.at[step], partner, tp
        )

    def cross(step, d):
        to = lax.rem(outer + d, outers)
        return remote(
            recv1.at[step, :, to], recv2.at[step, d - 1],
            s2_send.at[step, d - 1], s2_recv.at[step, d - 1], to * 2 + core, tp,
        )

    tile = 512

    def turn(step, carry):
        @pl.when((step >= 1) & (step < size))
        def _():
            for way in range(2):
                ring(step - 1, way).wait_recv()

        @pl.when(step < size - 1)
        def _():
            for way in range(2):
                ring(step, way).start()

        @pl.when((step >= 1) & (step <= size))
        def _():
            at = step - 1
            swap(at).wait()
            for d in range(1, outers):
                to = lax.rem(outer + d, outers)
                total = own[:, to] + recv1[at, :, to].astype(jnp.float32)
                recv1[at, :, to] = total.astype(jnp.bfloat16)
                cross(at, d).start()
            fin[at % 2] = own[:, outer] + recv1[at, :, outer].astype(jnp.float32)

        @pl.when(step >= 2)
        def _():
            at = step - 2
            for d in range(1, outers):
                cross(at, d).wait_recv()
            total = fin[at % 2]
            for d in range(1, outers):
                total = total + recv2[at, d - 1].astype(jnp.float32)
            total = total.astype(jnp.bfloat16)
            out_ref[2 * ring_index(place - at, size)] = total[0]
            out_ref[2 * ring_index(place + at, size) + 1] = total[1]

        @pl.when(step < size)
        def _():
            @pl.loop(0, width // tile)
            def _(n):
                columns = pl.ds(pl.multiple_of(n * tile, tile), tile)
                rows = act[step].reshape(2 * groups * seqs, depth)
                value = jnp.dot(rows, w_ref[:, columns], preferred_element_type=jnp.float32)
                value = value.reshape(2, outers, 2, seqs, tile)
                first, second = value[:, :, 0], value[:, :, 1]
                own[:, :, :, columns] = jnp.where(core == 0, first, second)
                send1[:, :, :, columns] = jnp.where(core == 0, second, first).astype(jnp.bfloat16)

            swap(step).start()

        return carry

    lax.fori_loop(0, size + 2, turn, 0)

    for copy in spread + handed:
        copy.wait_send()

    def drain(step, carry):
        @pl.when(step < size - 1)
        def _():
            for way in range(2):
                ring(step, way).wait_send()

        for d in range(1, outers):
            cross(step, d).wait_send()
        return carry

    lax.fori_loop(0, size, drain, 0)


def project(layout, hid, weights, groups, size):
    parts, steps, per_step, panel_rows = hid.shape
    depth, width = weights.shape
    seqs = steps * per_step // (2 * size)
    hid = hid.reshape(parts, 2 * size, seqs, panel_rows)
    outers = groups // 2
    bf16, f32 = jnp.bfloat16, jnp.float32
    dma = pltpu.SemaphoreType.DMA
    vmem = pl.BlockSpec(memory_space=pltpu.VMEM)
    out = pl.pallas_call(
        functools.partial(project_kernel, groups, size),
        out_shape=jax.ShapeDtypeStruct((2 * size, seqs, width), bf16),
        in_specs=[
            pl.BlockSpec(memory_space=pltpu.SMEM), vmem, pl.BlockSpec(memory_space=pl.ANY),
        ],
        out_specs=vmem,
        scratch_shapes=[
            pltpu.VMEM((depth, width), bf16),
            pltpu.VMEM((parts * size, 2, seqs, panel_rows), bf16),
            pltpu.VMEM((groups - 1, 2, seqs, depth), bf16),
            pltpu.VMEM((size, 2, groups, seqs, depth), bf16),
            pltpu.VMEM((2, outers, seqs, width), bf16),
            pltpu.VMEM((size, 2, outers, seqs, width), bf16),
            pltpu.VMEM((2, outers, seqs, width), f32),
            pltpu.VMEM((2, 2, seqs, width), f32),
            pltpu.VMEM((size, outers - 1, 2, seqs, width), bf16),
            dma(()),
            dma((size,)), dma((size,)),
            dma((groups,)), dma((groups,)),
            dma((size, 2)), dma((size, 2)),
            dma((size,)), dma((size,)),
            dma((size, outers - 1)), dma((size, outers - 1)),
        ],
        compiler_params=pltpu.CompilerParams(
            collective_id=0, has_side_effects=True, vmem_limit_bytes=58 * MIB
        ),
        cost_estimate=pl.CostEstimate(
            flops=4 * groups * size * seqs * depth * width,
            bytes_accessed=16 * MIB, transcendentals=0,
        ),
    )(layout, hid, weights)
    return out.reshape(steps, per_step, width)


def mix_kernel(
    size, x_ref, start_ref, cw_ref, cb_ref, xw_ref, xc_ref, low_ref, bc_ref,
    win, p_low, p_bc, g_low, g_bc, l_send, l_recv, c_send, c_recv, ol_send, ol_recv, oc_send, oc_recv,
):
    grp, tp = lax.axis_index("grp"), lax.axis_index("tp")
    steps, seqs, channels = xc_ref.shape
    taps = cw_ref.shape[0]
    rank = low_ref.shape[2]
    each = steps // size

    meet([(grp, lax.rem(tp + d, size)) for d in range(1, size)])

    win[: taps - 1] = start_ref[...]
    win[taps - 1 :] = x_ref[...].astype(jnp.float32)

    def conv(t, carry):
        total = jnp.broadcast_to(cb_ref[...], (seqs, channels))
        for tap in range(taps):
            total = total + cw_ref[tap : tap + 1, :] * win[t + tap]
        xc_ref[t] = (total * jax.nn.sigmoid(total)).astype(jnp.bfloat16)
        return carry

    lax.fori_loop(0, steps, conv, 0)

    def remote(src, dst, send, recv, to):
        return pltpu.make_async_remote_copy(
            src_ref=src, dst_ref=dst, send_sem=send, recv_sem=recv,
            device_id=(grp, to), device_id_type=MESH,
        )

    rows = xc_ref[...].reshape(steps * seqs, channels)
    part = jnp.dot(rows, xw_ref[...], preferred_element_type=jnp.float32)
    part = part.reshape(steps, seqs, xw_ref.shape[1])
    p_low[...] = part[:, :, :rank].astype(jnp.bfloat16)
    p_bc[...] = part[:, :, rank:]

    gathers = []
    for d in range(1, size):
        to = lax.rem(tp + d, size)
        span = pl.ds(each * to, each)
        for copy in (
            remote(p_low.at[span], g_low.at[d], l_send.at[d], l_recv.at[d], to),
            remote(p_bc.at[span], g_bc.at[d], c_send.at[d], c_recv.at[d], to),
        ):
            copy.start()
            gathers.append(copy)
    mine = pl.ds(each * tp, each)
    for copy in gathers:
        copy.wait_recv()
    low = p_low[mine].astype(jnp.float32)
    bc = p_bc[mine]
    for d in range(1, size):
        low = low + g_low[d].astype(jnp.float32)
        bc = bc + g_bc[d]
    low_ref[mine] = low.astype(jnp.bfloat16)
    bc_ref[mine] = bc
    shares = []
    for d in range(1, size):
        to = lax.rem(tp + d, size)
        for copy in (
            remote(low_ref.at[mine], low_ref.at[mine], ol_send.at[d], ol_recv.at[d], to),
            remote(bc_ref.at[mine], bc_ref.at[mine], oc_send.at[d], oc_recv.at[d], to),
        ):
            copy.start()
            shares.append(copy)
    for copy in shares:
        copy.wait_recv()
    for copy in gathers + shares:
        copy.wait_send()


def mix(xz, start, conv_weight, conv_bias, x_weight, rank, size):
    steps, seqs, both = xz.shape
    channels = both // 2
    extra = 128
    each = steps // size
    bf16, f32 = jnp.bfloat16, jnp.float32
    dma = pltpu.SemaphoreType.DMA
    vmem = pl.BlockSpec(memory_space=pltpu.VMEM)
    x_weight = jnp.pad(x_weight, ((0, 0), (0, rank + extra - x_weight.shape[1])))
    return pl.pallas_call(
        functools.partial(mix_kernel, size),
        grid=(1,),
        out_shape=(
            jax.ShapeDtypeStruct((steps, seqs, channels), bf16),
            jax.ShapeDtypeStruct((steps, seqs, rank), bf16),
            jax.ShapeDtypeStruct((steps, seqs, extra), f32),
        ),
        in_specs=[
            pl.BlockSpec((steps, seqs, channels), lambda i: (0, 0, 0)),
            vmem, vmem, vmem, vmem,
        ],
        out_specs=[vmem] * 3,
        scratch_shapes=[
            pltpu.VMEM((start.shape[0] + steps, seqs, channels), f32),
            pltpu.VMEM((steps, seqs, rank), bf16),
            pltpu.VMEM((steps, seqs, extra), f32),
            pltpu.VMEM((size, each, seqs, rank), bf16),
            pltpu.VMEM((size, each, seqs, extra), f32),
        ]
        + [dma((size,))] * 8,
        compiler_params=pltpu.CompilerParams(
            collective_id=1, has_side_effects=True, vmem_limit_bytes=40 * MIB
        ),
    )(xz, start, conv_weight, conv_bias.reshape(1, channels), x_weight)


def scan_kernel(
    last_ref, z_ref, xc_ref, low_ref, bc_ref, start_ref, dtw_ref, dtb_ref, rate_ref, skip_ref,
    mixed_ref, final_ref, step_ref,
):
    steps, seqs, channels = xc_ref.shape
    states = rate_ref.shape[0]
    tail = last_ref.shape[0]
    rows = low_ref[...].reshape(steps * seqs, low_ref.shape[2])
    drive = jnp.dot(rows, dtw_ref[...], preferred_element_type=jnp.float32) + dtb_ref[...]
    drive = jnp.maximum(drive, 0.0) + jnp.log1p(jnp.exp(-jnp.abs(drive)))
    step_ref[...] = drive.reshape(steps, seqs, channels)
    final_ref[:tail] = last_ref[...].astype(jnp.float32)
    final_ref[tail:] = start_ref[...]

    def advance(t, carry):
        step = step_ref[t]
        xc = xc_ref[t].astype(jnp.float32)
        bc = bc_ref[t]
        push = step * xc
        output = skip_ref[...] * xc
        for n in range(states):
            decay = jnp.exp(-step * rate_ref[n : n + 1, :])
            state = decay * final_ref[tail + n] + push * bc[:, n : n + 1]
            final_ref[tail + n] = state
            output = output + bc[:, states + n : states + n + 1] * state
        z = z_ref[t].astype(jnp.float32)
        mixed_ref[t] = (output * (z * jax.nn.sigmoid(z))).astype(jnp.bfloat16)
        return carry

    lax.fori_loop(0, steps, advance, 0)


def scan(xz, xc, low, bc, start, dt_weight, dt_bias, decay_rate, skip_gain, tail):
    steps, seqs, channels = xc.shape
    states = decay_rate.shape[0]
    rank = low.shape[2]
    block = 256
    count = channels // block
    return pl.pallas_call(
        scan_kernel,
        grid=(count,),
        out_shape=(
            jax.ShapeDtypeStruct((steps, seqs, channels), jnp.bfloat16),
            jax.ShapeDtypeStruct((tail + states, seqs, channels), jnp.float32),
        ),
        in_specs=[
            pl.BlockSpec((tail, seqs, block), lambda i: (0, 0, i)),
            pl.BlockSpec((steps, seqs, block), lambda i: (0, 0, count + i)),
            pl.BlockSpec((steps, seqs, block), lambda i: (0, 0, i)),
            pl.BlockSpec((steps, seqs, rank), lambda i: (0, 0, 0)),
            pl.BlockSpec((steps, seqs, bc.shape[2]), lambda i: (0, 0, 0)),
            pl.BlockSpec((states, seqs, block), lambda i: (0, 0, i)),
            pl.BlockSpec((rank, block), lambda i: (0, i)),
            pl.BlockSpec((1, block), lambda i: (0, i)),
            pl.BlockSpec((states, block), lambda i: (0, i)),
            pl.BlockSpec((1, block), lambda i: (0, i)),
        ],
        out_specs=[
            pl.BlockSpec((steps, seqs, block), lambda i: (0, 0, i)),
            pl.BlockSpec((tail + states, seqs, block), lambda i: (0, 0, i)),
        ],
        scratch_shapes=[pltpu.VMEM((steps, seqs, block), jnp.float32)],
        compiler_params=pltpu.CompilerParams(vmem_limit_bytes=40 * MIB),
    )(
        xz[steps - tail :, :, :channels], xz, xc, low, bc, start, dt_weight,
        dt_bias.reshape(1, channels), decay_rate, skip_gain.reshape(1, channels),
    )


def local(
    groups,
    size,
    in_panels,
    layout,
    hidden,
    prompt_state,
    fork_counts,
    conv_weight,
    conv_bias,
    x_weight,
    dt_weight,
    dt_bias,
    decay_rate,
    skip_gain,
):
    seqs, steps, features = hidden.shape
    panels, panel_rows, _, channels = in_panels.shape
    taps = conv_weight.shape[0]
    rank = dt_weight.shape[0]
    prompts = lax.all_gather(prompt_state, "grp", axis=0, tiled=True)
    weights = in_panels.reshape(panels * panel_rows, 2 * channels)
    hid = hidden.reshape(seqs, steps, features // panel_rows, panel_rows).transpose(2, 1, 0, 3)
    own_counts = lax.dynamic_slice_in_dim(fork_counts, lax.axis_index("grp"), 1, 0)
    sources = fork_sources(own_counts, seqs)[0]
    prompt_ids = jnp.arange(prompts.shape[0], dtype=jnp.int32)
    selector = (sources[:, None] == prompt_ids[None, :]).astype(jnp.float32)
    start = jnp.einsum("sp,pkc->ksc", selector, prompts, precision=lax.Precision.HIGHEST)
    xz = project(layout, hid, weights, groups, size)
    xc, low, bc = mix(xz, start[: taps - 1], conv_weight, conv_bias, x_weight, rank, size)
    mixed, final = scan(
        xz, xc, low, bc, start[taps - 1 :], dt_weight, dt_bias, decay_rate, skip_gain, taps - 1
    )
    return mixed.transpose(1, 0, 2), final.transpose(1, 0, 2)


def solution(mesh):
    return jax.shard_map(
        functools.partial(local, mesh.shape["grp"], mesh.shape["tp"]),
        mesh=mesh,
        in_specs=(
            P("grp", None, None, "tp"),
            P(),
            P("grp", None, "tp"),
            P("grp", None, "tp"),
            P(),
            P(None, "tp"),
            P("tp"),
            P("tp", None),
            P(None, "tp"),
            P("tp"),
            P(None, "tp"),
            P("tp"),
        ),
        out_specs=(P("grp", None, "tp"), P("grp", None, "tp")),
        check_vma=False,
    )
```

```python
import functools
import math

import jax
import jax.numpy as jnp
from jax import lax
from jax.experimental import pallas as pl
from jax.experimental.pallas import tpu as pltpu
from jax.sharding import PartitionSpec as P

MESH = pl.DeviceIdType.MESH
MIB = 1024 * 1024


def fork_sources(counts, per_group):
    running = jnp.cumsum(counts, axis=1)
    slot_ids = jnp.arange(per_group, dtype=jnp.int32)
    return jnp.sum((running[:, None, :] <= slot_ids[None, :, None]).astype(jnp.int32), axis=2)


def ring_place(index, size):
    major, minor = index // 2, index % 2
    return jnp.where(minor == 0, major, size - 1 - major)


def ring_index(place, size):
    place = lax.rem(place + 2 * size, size)
    return jnp.where(place < size // 2, 2 * place, 2 * (size - 1 - place) + 1)


def meet(peers):
    barrier = pltpu.get_barrier_semaphore()
    for peer in peers:
        pl.semaphore_signal(barrier, inc=1, device_id=peer, device_id_type=MESH)
    pl.semaphore_wait(barrier, len(peers))


def project_kernel(
    groups, size, layout_ref, hid_ref, w_hbm, out_ref,
    w_ref, blocks, picked, act, send1, recv1, own, fin, recv2,
    w_sem, a_send, a_recv, b_send, b_recv, r_send, r_recv, s1_send, s1_recv, s2_send, s2_recv,
):
    grp, tp = lax.axis_index("grp"), lax.axis_index("tp")
    outers = groups // 2
    outer, core = grp // 2, grp % 2
    partner = outer * 2 + 1 - core
    parts, _, seqs, panel_rows = hid_ref.shape
    depth = 2 * panel_rows
    width = w_ref.shape[1]
    place = ring_place(tp, size)
    right, left = ring_index(place + 1, size), ring_index(place - 1, size)

    def remote(src, dst, send, recv, g, t):
        return pltpu.make_async_remote_copy(
            src_ref=src, dst_ref=dst, send_sem=send, recv_sem=recv,
            device_id=(g, t), device_id_type=MESH,
        )

    load_w = pltpu.make_async_copy(w_hbm, w_ref, w_sem)
    load_w.start()
    meet(
        [(grp, lax.rem(tp + d, size)) for d in range(1, size)]
        + [(lax.rem(grp + d, groups), tp) for d in range(1, groups)]
    )

    spread = []
    for d in range(1, size):
        to = lax.rem(tp + d, size)
        copy = remote(
            hid_ref.at[:, pl.ds(2 * to, 2)], blocks.at[pl.ds(tp * parts, parts)],
            a_send.at[d], a_recv.at[d], grp, to,
        )
        copy.start()
        spread.append(copy)
    blocks[pl.ds(tp * parts, parts)] = hid_ref[:, pl.ds(2 * tp, 2)]
    for copy in spread:
        copy.wait_recv()

    handed = []
    for d in range(1, groups + 1):
        to = lax.rem(grp + d, groups)
        for j in range(2):
            block = blocks[layout_ref[2 * to + j]]
            columns = slice(j * panel_rows, (j + 1) * panel_rows)
            if d < groups:
                picked[d - 1, :, :, columns] = block
            else:
                act[0, :, grp, :, columns] = block
        if d < groups:
            copy = remote(
                picked.at[d - 1], act.at[0, :, grp], b_send.at[d], b_recv.at[d], to, tp
            )
            copy.start()
            handed.append(copy)
    load_w.wait()
    for copy in handed:
        copy.wait_recv()

    def ring(step, way):
        return remote(
            act.at[step, way], act.at[step + 1, way],
            r_send.at[step, way], r_recv.at[step, way], grp, (right, left)[way],
        )

    def swap(step):
        return remote(
            send1, recv1.at[step], s1_send.at[step], s1_recv.at[step], partner, tp
        )

    def cross(step, d):
        to = lax.rem(outer + d, outers)
        return remote(
            recv1.at[step, :, to], recv2.at[step, d - 1],
            s2_send.at[step, d - 1], s2_recv.at[step, d - 1], to * 2 + core, tp,
        )

    tile = 512

    def turn(step, carry):
        @pl.when((step >= 1) & (step < size))
        def _():
            for way in range(2):
                ring(step - 1, way).wait_recv()

        @pl.when(step < size - 1)
        def _():
            for way in range(2):
                ring(step, way).start()

        @pl.when((step >= 1) & (step <= size))
        def _():
            at = step - 1
            swap(at).wait()
            for d in range(1, outers):
                to = lax.rem(outer + d, outers)
                total = own[:, to] + recv1[at, :, to].astype(jnp.float32)
                recv1[at, :, to] = total.astype(jnp.bfloat16)
                cross(at, d).start()
            fin[at % 2] = own[:, outer] + recv1[at, :, outer].astype(jnp.float32)

        @pl.when(step >= 2)
        def _():
            at = step - 2
            for d in range(1, outers):
                cross(at, d).wait_recv()
            total = fin[at % 2]
            for d in range(1, outers):
                total = total + recv2[at, d - 1].astype(jnp.float32)
            total = total.astype(jnp.bfloat16)
            out_ref[2 * ring_index(place - at, size)] = total[0]
            out_ref[2 * ring_index(place + at, size) + 1] = total[1]

        @pl.when(step < size)
        def _():
            @pl.loop(0, width // tile)
            def _(n):
                columns = pl.ds(pl.multiple_of(n * tile, tile), tile)
                rows = act[step].reshape(2 * groups * seqs, depth)
                value = jnp.dot(rows, w_ref[:, columns], preferred_element_type=jnp.float32)
                value = value.reshape(2, outers, 2, seqs, tile)
                first, second = value[:, :, 0], value[:, :, 1]
                own[:, :, :, columns] = jnp.where(core == 0, first, second)
                send1[:, :, :, columns] = jnp.where(core == 0, second, first).astype(jnp.bfloat16)

            swap(step).start()

        return carry

    lax.fori_loop(0, size + 2, turn, 0)

    for copy in spread + handed:
        copy.wait_send()

    def drain(step, carry):
        @pl.when(step < size - 1)
        def _():
            for way in range(2):
                ring(step, way).wait_send()

        for d in range(1, outers):
            cross(step, d).wait_send()
        return carry

    lax.fori_loop(0, size, drain, 0)


def project(layout, hid, weights, groups, size):
    parts, steps, per_step, panel_rows = hid.shape
    depth, width = weights.shape
    seqs = steps * per_step // (2 * size)
    hid = hid.reshape(parts, 2 * size, seqs, panel_rows)
    outers = groups // 2
    bf16, f32 = jnp.bfloat16, jnp.float32
    dma = pltpu.SemaphoreType.DMA
    vmem = pl.BlockSpec(memory_space=pltpu.VMEM)
    out = pl.pallas_call(
        functools.partial(project_kernel, groups, size),
        out_shape=jax.ShapeDtypeStruct((2 * size, seqs, width), bf16),
        in_specs=[
            pl.BlockSpec(memory_space=pltpu.SMEM), vmem, pl.BlockSpec(memory_space=pl.ANY),
        ],
        out_specs=vmem,
        scratch_shapes=[
            pltpu.VMEM((depth, width), bf16),
            pltpu.VMEM((parts * size, 2, seqs, panel_rows), bf16),
            pltpu.VMEM((groups - 1, 2, seqs, depth), bf16),
            pltpu.VMEM((size, 2, groups, seqs, depth), bf16),
            pltpu.VMEM((2, outers, seqs, width), bf16),
            pltpu.VMEM((size, 2, outers, seqs, width), bf16),
            pltpu.VMEM((2, outers, seqs, width), f32),
            pltpu.VMEM((2, 2, seqs, width), f32),
            pltpu.VMEM((size, outers - 1, 2, seqs, width), bf16),
            dma(()),
            dma((size,)), dma((size,)),
            dma((groups,)), dma((groups,)),
            dma((size, 2)), dma((size, 2)),
            dma((size,)), dma((size,)),
            dma((size, outers - 1)), dma((size, outers - 1)),
        ],
        compiler_params=pltpu.CompilerParams(
            collective_id=0, has_side_effects=True, vmem_limit_bytes=58 * MIB
        ),
        cost_estimate=pl.CostEstimate(
            flops=4 * groups * size * seqs * depth * width,
            bytes_accessed=16 * MIB, transcendentals=0,
        ),
    )(layout, hid, weights)
    return out.reshape(steps, per_step, width)


def mix_kernel(
    size, x_ref, start_ref, cw_ref, cb_ref, xw_ref, xc_ref, low_ref, bc_ref,
    win, p_low, p_bc, g_low, g_bc, l_send, l_recv, c_send, c_recv, ol_send, ol_recv, oc_send, oc_recv,
):
    grp, tp = lax.axis_index("grp"), lax.axis_index("tp")
    steps, seqs, channels = xc_ref.shape
    taps = cw_ref.shape[0]
    rank = low_ref.shape[2]
    each = steps // size

    meet([(grp, lax.rem(tp + d, size)) for d in range(1, size)])

    win[: taps - 1] = start_ref[...]
    win[taps - 1 :] = x_ref[...].astype(jnp.float32)

    def remote(src, dst, send, recv, to):
        return pltpu.make_async_remote_copy(
            src_ref=src, dst_ref=dst, send_sem=send, recv_sem=recv,
            device_id=(grp, to), device_id_type=MESH,
        )

    def conv(first):
        total = jnp.broadcast_to(cb_ref[...], (each, seqs, channels))
        for tap in range(taps):
            total = total + cw_ref[tap : tap + 1, :] * win[pl.ds(first + tap, each)]
        value = (total * jax.nn.sigmoid(total)).astype(jnp.bfloat16)
        xc_ref[pl.ds(first, each)] = value
        return value.reshape(each * seqs, channels)

    lanes = lax.broadcasted_iota(jnp.int32, (each, 8, xw_ref.shape[1] - rank), 2)
    quarter = (xw_ref.shape[1] - rank) * 8 // seqs
    gathers = []
    half = size // 2
    for part in range(2):
        offsets = range(1 + part * half, 1 + (part + 1) * half)
        rows = jnp.concatenate([conv(each * lax.rem(tp + d, size)) for d in offsets], axis=0)
        product = jnp.dot(rows, xw_ref[...], preferred_element_type=jnp.float32)
        product = product.reshape(half, each, seqs, xw_ref.shape[1])
        for i, d in enumerate(offsets):
            to = lax.rem(tp + d, size)
            span = pl.ds(each * to, each)
            p_low[span] = product[i, :, :, :rank].astype(jnp.bfloat16)
            packed = product[i, :, :8, rank:]
            for q in range(1, seqs // 8):
                packed = jnp.where(
                    lanes < q * quarter, packed, product[i, :, q * 8 : q * 8 + 8, rank:]
                )
            p_bc[span] = packed
            if d == size:
                continue
            for copy in (
                remote(p_low.at[span], g_low.at[d], l_send.at[d], l_recv.at[d], to),
                remote(p_bc.at[span], g_bc.at[d], c_send.at[d], c_recv.at[d], to),
            ):
                copy.start()
                gathers.append(copy)
    mine = pl.ds(each * tp, each)
    for copy in gathers:
        copy.wait_recv()
    low = p_low[mine].astype(jnp.float32)
    bc = p_bc[mine]
    for d in range(1, size):
        low = low + g_low[d].astype(jnp.float32)
        bc = bc + g_bc[d]
    low_ref[mine] = low.astype(jnp.bfloat16)
    bc_ref[mine] = bc
    shares = []
    for d in range(1, size):
        to = lax.rem(tp + d, size)
        for copy in (
            remote(low_ref.at[mine], low_ref.at[mine], ol_send.at[d], ol_recv.at[d], to),
            remote(bc_ref.at[mine], bc_ref.at[mine], oc_send.at[d], oc_recv.at[d], to),
        ):
            copy.start()
            shares.append(copy)
    for copy in shares:
        copy.wait_recv()
    for copy in gathers + shares:
        copy.wait_send()


def mix(xz, start, conv_weight, conv_bias, x_weight, rank, size):
    steps, seqs, both = xz.shape
    channels = both // 2
    repeats = seqs // 8
    extra = (x_weight.shape[1] - rank) * repeats
    each = steps // size
    bf16, f32 = jnp.bfloat16, jnp.float32
    dma = pltpu.SemaphoreType.DMA
    vmem = pl.BlockSpec(memory_space=pltpu.VMEM)
    x_weight = jnp.concatenate(
        [x_weight[:, :rank], jnp.tile(x_weight[:, rank:], (1, repeats))], axis=1
    )
    return pl.pallas_call(
        functools.partial(mix_kernel, size),
        grid=(1,),
        out_shape=(
            jax.ShapeDtypeStruct((steps, seqs, channels), bf16),
            jax.ShapeDtypeStruct((steps, seqs, rank), bf16),
            jax.ShapeDtypeStruct((steps, 8, extra), f32),
        ),
        in_specs=[
            pl.BlockSpec((steps, seqs, channels), lambda i: (0, 0, 0)),
            vmem, vmem, vmem, vmem,
        ],
        out_specs=[vmem] * 3,
        scratch_shapes=[
            pltpu.VMEM((start.shape[0] + steps, seqs, channels), f32),
            pltpu.VMEM((steps, seqs, rank), bf16),
            pltpu.VMEM((steps, 8, extra), f32),
            pltpu.VMEM((size, each, seqs, rank), bf16),
            pltpu.VMEM((size, each, 8, extra), f32),
        ]
        + [dma((size,))] * 8,
        compiler_params=pltpu.CompilerParams(
            collective_id=1, has_side_effects=True, vmem_limit_bytes=40 * MIB
        ),
    )(xz, start, conv_weight, conv_bias.reshape(1, channels), x_weight)


def scan_kernel(
    last_ref, z_ref, xc_ref, low_ref, bc_ref, start_ref, dtw_ref, dtb_ref, rate_ref, skip_ref,
    mixed_ref, final_ref, step_ref,
):
    steps, seqs, channels = xc_ref.shape
    states = rate_ref.shape[0]
    tail = last_ref.shape[0]
    rows = low_ref[...].reshape(steps * seqs, low_ref.shape[2])
    drive = jnp.dot(rows, dtw_ref[...], preferred_element_type=jnp.float32) + dtb_ref[...]
    drive = jnp.maximum(drive, 0.0) + jnp.log1p(jnp.exp(-jnp.abs(drive)))
    step_ref[...] = drive.reshape(steps, seqs, channels)
    final_ref[:tail] = last_ref[...].astype(jnp.float32)
    final_ref[tail:] = start_ref[...]

    rate = rate_ref[...] * -math.log2(math.e)
    pairs = 2 * states

    def advance(t, carry):
        step_all = step_ref[t]
        xc_all = xc_ref[t].astype(jnp.float32)
        z = z_ref[t].astype(jnp.float32)
        gate = z * jax.nn.sigmoid(z)
        bc = bc_ref[t]
        outputs = []
        for q in range(seqs // 8):
            own = slice(q * 8, q * 8 + 8)
            step, xc = step_all[own], xc_all[own]
            push = step * xc
            output = skip_ref[...] * xc
            for n in range(states):
                b_at, c_at = q * pairs + n, q * pairs + states + n
                state = (
                    jnp.exp2(step * rate[n : n + 1, :]) * final_ref[tail + n, own]
                    + push * bc[:, b_at : b_at + 1]
                )
                final_ref[tail + n, own] = state
                output = output + bc[:, c_at : c_at + 1] * state
            outputs.append(output)
        mixed_ref[t] = (jnp.concatenate(outputs, axis=0) * gate).astype(jnp.bfloat16)
        return carry

    lax.fori_loop(0, steps, advance, 0)


def scan(xz, xc, low, bc, start, dt_weight, dt_bias, decay_rate, skip_gain, tail):
    steps, seqs, channels = xc.shape
    states = decay_rate.shape[0]
    rank = low.shape[2]
    block = min(channels, 512)
    count = channels // block
    return pl.pallas_call(
        scan_kernel,
        grid=(count,),
        out_shape=(
            jax.ShapeDtypeStruct((steps, seqs, channels), jnp.bfloat16),
            jax.ShapeDtypeStruct((tail + states, seqs, channels), jnp.float32),
        ),
        in_specs=[
            pl.BlockSpec((tail, seqs, block), lambda i: (0, 0, i)),
            pl.BlockSpec((steps, seqs, block), lambda i: (0, 0, count + i)),
            pl.BlockSpec((steps, seqs, block), lambda i: (0, 0, i)),
            pl.BlockSpec((steps, seqs, rank), lambda i: (0, 0, 0)),
            pl.BlockSpec(bc.shape, lambda i: (0, 0, 0)),
            pl.BlockSpec((states, seqs, block), lambda i: (0, 0, i)),
            pl.BlockSpec((rank, block), lambda i: (0, i)),
            pl.BlockSpec((1, block), lambda i: (0, i)),
            pl.BlockSpec((states, block), lambda i: (0, i)),
            pl.BlockSpec((1, block), lambda i: (0, i)),
        ],
        out_specs=[
            pl.BlockSpec((steps, seqs, block), lambda i: (0, 0, i)),
            pl.BlockSpec((tail + states, seqs, block), lambda i: (0, 0, i)),
        ],
        scratch_shapes=[pltpu.VMEM((steps, seqs, block), jnp.float32)],
        compiler_params=pltpu.CompilerParams(vmem_limit_bytes=40 * MIB),
    )(
        xz[steps - tail :, :, :channels], xz, xc, low, bc, start, dt_weight,
        dt_bias.reshape(1, channels), decay_rate, skip_gain.reshape(1, channels),
    )


def local(
    groups,
    size,
    in_panels,
    layout,
    hidden,
    prompt_state,
    fork_counts,
    conv_weight,
    conv_bias,
    x_weight,
    dt_weight,
    dt_bias,
    decay_rate,
    skip_gain,
):
    seqs, steps, features = hidden.shape
    panels, panel_rows, _, channels = in_panels.shape
    taps = conv_weight.shape[0]
    rank = dt_weight.shape[0]
    prompts = lax.all_gather(prompt_state, "grp", axis=0, tiled=True)
    weights = in_panels.reshape(panels * panel_rows, 2 * channels)
    hid = hidden.reshape(seqs, steps, features // panel_rows, panel_rows).transpose(2, 1, 0, 3)
    own_counts = lax.dynamic_slice_in_dim(fork_counts, lax.axis_index("grp"), 1, 0)
    sources = fork_sources(own_counts, seqs)[0]
    prompt_ids = jnp.arange(prompts.shape[0], dtype=jnp.int32)
    selector = (sources[:, None] == prompt_ids[None, :]).astype(jnp.float32)
    start = jnp.einsum("sp,pkc->ksc", selector, prompts, precision=lax.Precision.HIGHEST)
    xz = project(layout, hid, weights, groups, size)
    xc, low, bc = mix(xz, start[: taps - 1], conv_weight, conv_bias, x_weight, rank, size)
    mixed, final = scan(
        xz, xc, low, bc, start[taps - 1 :], dt_weight, dt_bias, decay_rate, skip_gain, taps - 1
    )
    return mixed.transpose(1, 0, 2), final.transpose(1, 0, 2)


def solution(mesh):
    return jax.shard_map(
        functools.partial(local, mesh.shape["grp"], mesh.shape["tp"]),
        mesh=mesh,
        in_specs=(
            P("grp", None, None, "tp"),
            P(),
            P("grp", None, "tp"),
            P("grp", None, "tp"),
            P(),
            P(None, "tp"),
            P("tp"),
            P("tp", None),
            P(None, "tp"),
            P("tp"),
            P(None, "tp"),
            P("tp"),
        ),
        out_specs=(P("grp", None, "tp"), P("grp", None, "tp")),
        check_vma=False,
    )
```

```python
import functools
import math

import jax
import jax.numpy as jnp
from jax import lax
from jax.experimental import pallas as pl
from jax.experimental.pallas import tpu as pltpu
from jax.sharding import PartitionSpec as P

MESH = pl.DeviceIdType.MESH
MIB = 1024 * 1024


def fork_sources(counts, per_group):
    running = jnp.cumsum(counts, axis=1)
    slot_ids = jnp.arange(per_group, dtype=jnp.int32)
    return jnp.sum((running[:, None, :] <= slot_ids[None, :, None]).astype(jnp.int32), axis=2)


def ring_place(index, size):
    major, minor = index // 2, index % 2
    return jnp.where(minor == 0, major, size - 1 - major)


def ring_index(place, size):
    place = lax.rem(place + 2 * size, size)
    return jnp.where(place < size // 2, 2 * place, 2 * (size - 1 - place) + 1)


def meet(peers):
    barrier = pltpu.get_barrier_semaphore()
    for peer in peers:
        pl.semaphore_signal(barrier, inc=1, device_id=peer, device_id_type=MESH)
    pl.semaphore_wait(barrier, len(peers))


def project_kernel(
    groups, size, layout_ref, hid_ref, w_hbm, out_ref,
    w_ref, raw, blocks_a, blocks_b, picked, act, send1, recv1, own, fin, recv2,
    w_sem, a_send, a_recv, b_send, b_recv, r_send, r_recv, s1_send, s1_recv, s2_send, s2_recv,
):
    grp, tp = lax.axis_index("grp"), lax.axis_index("tp")
    outers = groups // 2
    outer, core = grp // 2, grp % 2
    partner = outer * 2 + 1 - core
    parts, _, seqs, panel_rows = hid_ref.shape
    depth = 2 * panel_rows
    width = w_ref.shape[1]
    place = ring_place(tp, size)
    right, left = ring_index(place + 1, size), ring_index(place - 1, size)

    def remote(src, dst, send, recv, g, t):
        return pltpu.make_async_remote_copy(
            src_ref=src, dst_ref=dst, send_sem=send, recv_sem=recv,
            device_id=(g, t), device_id_type=MESH,
        )

    load_w = pltpu.make_async_copy(w_hbm, raw, w_sem)
    load_w.start()
    meet(
        [(grp, lax.rem(tp + d, size)) for d in range(1, size)]
        + [(lax.rem(grp + d, groups), tp) for d in range(1, groups)]
    )

    blocks = (blocks_a, blocks_b)
    spread = ([], [])
    for way in range(2):
        for d in range(1, size):
            to = lax.rem(tp + d, size)
            copy = remote(
                hid_ref.at[:, 2 * to + way], blocks[way].at[pl.ds(tp * parts, parts)],
                a_send.at[way, d], a_recv.at[way, d], grp, to,
            )
            copy.start()
            spread[way].append(copy)
        blocks[way][pl.ds(tp * parts, parts)] = hid_ref[:, 2 * tp + way]

    load_w.wait()
    run = 2 * width // 256 * 16
    kinds = run // 16
    order = lax.broadcasted_iota(jnp.int32, (run, run), 0)
    source = lax.broadcasted_iota(jnp.int32, (run, run), 1)
    wanted = (order % 16) * kinds + (order // 16)
    sort = (source == wanted).astype(jnp.bfloat16)

    @pl.loop(0, depth // 32)
    def _(at):
        pair = jnp.concatenate(
            [raw[pl.ds(pl.multiple_of((2 * at + i) * run, run), run)] for i in range(2)], axis=1
        )
        tidy = jnp.dot(sort, pair, preferred_element_type=jnp.float32).astype(jnp.bfloat16)
        for i in range(2):
            rows = pl.ds(pl.multiple_of((2 * at + i) * 16, 16), 16)
            for kind in range(kinds):
                column = (kind % 2) * (width // 2) + (kind // 2) * 128
                w_ref[rows, column : column + 128] = tidy[
                    kind * 16 : kind * 16 + 16, i * 128 : i * 128 + 128
                ]

    def ring(step, way):
        return remote(
            act.at[step, way], act.at[step + 1, way],
            r_send.at[step, way], r_recv.at[step, way], grp, (right, left)[way],
        )

    handed = ([], [])
    for way in range(2):
        for copy in spread[way]:
            copy.wait_recv()
        for d in range(1, groups + 1):
            to = lax.rem(grp + d, groups)
            for j in range(2):
                block = blocks[way][layout_ref[2 * to + j]]
                columns = slice(j * panel_rows, (j + 1) * panel_rows)
                if d < groups:
                    picked[d - 1, way, :, columns] = block
                else:
                    act[0, way, grp, :, columns] = block
            if d < groups:
                copy = remote(
                    picked.at[d - 1, way], act.at[0, way, grp],
                    b_send.at[way, d], b_recv.at[way, d], to, tp,
                )
                copy.start()
                handed[way].append(copy)
    for way in range(2):
        for copy in handed[way]:
            copy.wait_recv()
        ring(0, way).start()

    def swap(step):
        return remote(
            send1, recv1.at[step], s1_send.at[step], s1_recv.at[step], partner, tp
        )

    def cross(step, d):
        to = lax.rem(outer + d, outers)
        return remote(
            recv1.at[step, :, to], recv2.at[step, d - 1],
            s2_send.at[step, d - 1], s2_recv.at[step, d - 1], to * 2 + core, tp,
        )

    tile = 512

    def turn(step, carry):
        @pl.when((step >= 1) & (step < size))
        def _():
            for way in range(2):
                ring(step - 1, way).wait_recv()

                @pl.when(step < size - 1)
                def _():
                    ring(step, way).start()

        @pl.when((step >= 1) & (step <= size))
        def _():
            at = step - 1
            swap(at).wait()
            for d in range(1, outers):
                to = lax.rem(outer + d, outers)
                total = own[:, to] + recv1[at, :, to].astype(jnp.float32)
                recv1[at, :, to] = total.astype(jnp.bfloat16)
                cross(at, d).start()
            fin[at % 2] = own[:, outer] + recv1[at, :, outer].astype(jnp.float32)

        @pl.when(step >= 2)
        def _():
            at = step - 2
            for d in range(1, outers):
                cross(at, d).wait_recv()
            total = fin[at % 2]
            for d in range(1, outers):
                total = total + recv2[at, d - 1].astype(jnp.float32)
            total = total.astype(jnp.bfloat16)
            out_ref[2 * ring_index(place - at, size)] = total[0]
            out_ref[2 * ring_index(place + at, size) + 1] = total[1]

        @pl.when(step < size)
        def _():
            @pl.loop(0, width // tile)
            def _(n):
                columns = pl.ds(pl.multiple_of(n * tile, tile), tile)
                rows = act[step].reshape(2 * groups * seqs, depth)
                value = jnp.dot(rows, w_ref[:, columns], preferred_element_type=jnp.float32)
                value = value.reshape(2, outers, 2, seqs, tile)
                first, second = value[:, :, 0], value[:, :, 1]
                own[:, :, :, columns] = jnp.where(core == 0, first, second)
                send1[:, :, :, columns] = jnp.where(core == 0, second, first).astype(jnp.bfloat16)

            swap(step).start()

        return carry

    lax.fori_loop(0, size + 2, turn, 0)

    for copy in spread[0] + spread[1] + handed[0] + handed[1]:
        copy.wait_send()

    def drain(step, carry):
        @pl.when(step < size - 1)
        def _():
            for way in range(2):
                ring(step, way).wait_send()

        for d in range(1, outers):
            cross(step, d).wait_send()
        return carry

    lax.fori_loop(0, size, drain, 0)


def project(layout, hid, weights, groups, size):
    parts, steps, per_step, panel_rows = hid.shape
    depth, width = 2 * panel_rows, weights.shape[0] * 128 // (2 * panel_rows)
    seqs = steps * per_step // (2 * size)
    hid = hid.reshape(parts, 2 * size, seqs, panel_rows)
    outers = groups // 2
    bf16, f32 = jnp.bfloat16, jnp.float32
    dma = pltpu.SemaphoreType.DMA
    vmem = pl.BlockSpec(memory_space=pltpu.VMEM)
    out = pl.pallas_call(
        functools.partial(project_kernel, groups, size),
        out_shape=jax.ShapeDtypeStruct((2 * size, seqs, width), bf16),
        in_specs=[
            pl.BlockSpec(memory_space=pltpu.SMEM), vmem, pl.BlockSpec(memory_space=pl.ANY),
        ],
        out_specs=vmem,
        scratch_shapes=[
            pltpu.VMEM((depth, width), bf16),
            pltpu.VMEM(weights.shape, bf16),
            pltpu.VMEM((parts * size, seqs, panel_rows), bf16),
            pltpu.VMEM((parts * size, seqs, panel_rows), bf16),
            pltpu.VMEM((groups - 1, 2, seqs, depth), bf16),
            pltpu.VMEM((size, 2, groups, seqs, depth), bf16),
            pltpu.VMEM((2, outers, seqs, width), bf16),
            pltpu.VMEM((size, 2, outers, seqs, width), bf16),
            pltpu.VMEM((2, outers, seqs, width), f32),
            pltpu.VMEM((2, 2, seqs, width), f32),
            pltpu.VMEM((size, outers - 1, 2, seqs, width), bf16),
            dma(()),
            dma((2, size)), dma((2, size)),
            dma((2, groups)), dma((2, groups)),
            dma((size, 2)), dma((size, 2)),
            dma((size,)), dma((size,)),
            dma((size, outers - 1)), dma((size, outers - 1)),
        ],
        compiler_params=pltpu.CompilerParams(
            collective_id=0, has_side_effects=True, vmem_limit_bytes=58 * MIB
        ),
        cost_estimate=pl.CostEstimate(
            flops=4 * groups * size * seqs * depth * width,
            bytes_accessed=16 * MIB, transcendentals=0,
        ),
    )(layout, hid, weights)
    return out.reshape(steps, per_step, width)


def mix_kernel(
    size, x_ref, start_ref, cw_ref, cb_ref, xw_ref, xc_ref, low_ref, bc_ref,
    win, p_low, p_bc, g_low, g_bc, l_send, l_recv, c_send, c_recv, ol_send, ol_recv, oc_send, oc_recv,
):
    grp, tp = lax.axis_index("grp"), lax.axis_index("tp")
    steps, seqs, channels = xc_ref.shape
    taps = cw_ref.shape[0]
    rank = low_ref.shape[2]
    each = steps // size

    meet([(grp, lax.rem(tp + d, size)) for d in range(1, size)])

    win[: taps - 1] = start_ref[...]
    win[taps - 1 :] = x_ref[...].astype(jnp.float32)

    def remote(src, dst, send, recv, to):
        return pltpu.make_async_remote_copy(
            src_ref=src, dst_ref=dst, send_sem=send, recv_sem=recv,
            device_id=(grp, to), device_id_type=MESH,
        )

    def conv(first):
        total = jnp.broadcast_to(cb_ref[...], (each, seqs, channels))
        for tap in range(taps):
            total = total + cw_ref[tap : tap + 1, :] * win[pl.ds(first + tap, each)]
        value = (total * jax.nn.sigmoid(total)).astype(jnp.bfloat16)
        xc_ref[pl.ds(first, each)] = value
        return value.reshape(each * seqs, channels)

    lanes = lax.broadcasted_iota(jnp.int32, (each, 8, xw_ref.shape[1] - rank), 2)
    quarter = (xw_ref.shape[1] - rank) * 8 // seqs
    gathers = []
    half = size // 2
    for part in range(2):
        offsets = range(1 + part * half, 1 + (part + 1) * half)
        rows = jnp.concatenate([conv(each * lax.rem(tp + d, size)) for d in offsets], axis=0)
        product = jnp.dot(rows, xw_ref[...], preferred_element_type=jnp.float32)
        product = product.reshape(half, each, seqs, xw_ref.shape[1])
        for i, d in enumerate(offsets):
            to = lax.rem(tp + d, size)
            span = pl.ds(each * to, each)
            p_low[span] = product[i, :, :, :rank].astype(jnp.bfloat16)
            packed = product[i, :, :8, rank:]
            for q in range(1, seqs // 8):
                packed = jnp.where(
                    lanes < q * quarter, packed, product[i, :, q * 8 : q * 8 + 8, rank:]
                )
            p_bc[span] = packed
            if d == size:
                continue
            for copy in (
                remote(p_low.at[span], g_low.at[d], l_send.at[d], l_recv.at[d], to),
                remote(p_bc.at[span], g_bc.at[d], c_send.at[d], c_recv.at[d], to),
            ):
                copy.start()
                gathers.append(copy)
    mine = pl.ds(each * tp, each)
    for copy in gathers:
        copy.wait_recv()
    low = p_low[mine].astype(jnp.float32)
    bc = p_bc[mine]
    for d in range(1, size):
        low = low + g_low[d].astype(jnp.float32)
        bc = bc + g_bc[d]
    low_ref[mine] = low.astype(jnp.bfloat16)
    bc_ref[mine] = bc
    shares = []
    for d in range(1, size):
        to = lax.rem(tp + d, size)
        for copy in (
            remote(low_ref.at[mine], low_ref.at[mine], ol_send.at[d], ol_recv.at[d], to),
            remote(bc_ref.at[mine], bc_ref.at[mine], oc_send.at[d], oc_recv.at[d], to),
        ):
            copy.start()
            shares.append(copy)
    for copy in shares:
        copy.wait_recv()
    for copy in gathers + shares:
        copy.wait_send()


def mix(xz, start, conv_weight, conv_bias, x_weight, rank, size):
    steps, seqs, both = xz.shape
    channels = both // 2
    repeats = seqs // 8
    extra = (x_weight.shape[1] - rank) * repeats
    each = steps // size
    bf16, f32 = jnp.bfloat16, jnp.float32
    dma = pltpu.SemaphoreType.DMA
    vmem = pl.BlockSpec(memory_space=pltpu.VMEM)
    x_weight = jnp.concatenate(
        [x_weight[:, :rank], jnp.tile(x_weight[:, rank:], (1, repeats))], axis=1
    )
    return pl.pallas_call(
        functools.partial(mix_kernel, size),
        grid=(1,),
        out_shape=(
            jax.ShapeDtypeStruct((steps, seqs, channels), bf16),
            jax.ShapeDtypeStruct((steps, seqs, rank), bf16),
            jax.ShapeDtypeStruct((steps, 8, extra), f32),
        ),
        in_specs=[
            pl.BlockSpec((steps, seqs, channels), lambda i: (0, 0, 0)),
            vmem, vmem, vmem, vmem,
        ],
        out_specs=[vmem] * 3,
        scratch_shapes=[
            pltpu.VMEM((start.shape[0] + steps, seqs, channels), f32),
            pltpu.VMEM((steps, seqs, rank), bf16),
            pltpu.VMEM((steps, 8, extra), f32),
            pltpu.VMEM((size, each, seqs, rank), bf16),
            pltpu.VMEM((size, each, 8, extra), f32),
        ]
        + [dma((size,))] * 8,
        compiler_params=pltpu.CompilerParams(
            collective_id=1, has_side_effects=True, vmem_limit_bytes=40 * MIB
        ),
    )(xz, start, conv_weight, conv_bias.reshape(1, channels), x_weight)


def scan_kernel(
    last_ref, z_ref, xc_ref, low_ref, bc_ref, start_ref, dtw_ref, dtb_ref, rate_ref, skip_ref,
    mixed_ref, final_ref, step_ref,
):
    steps, seqs, channels = xc_ref.shape
    states = rate_ref.shape[0]
    tail = last_ref.shape[0]
    rows = low_ref[...].reshape(steps * seqs, low_ref.shape[2])
    drive = jnp.dot(rows, dtw_ref[...], preferred_element_type=jnp.float32) + dtb_ref[...]
    drive = jnp.maximum(drive, 0.0) + jnp.log1p(jnp.exp(-jnp.abs(drive)))
    step_ref[...] = drive.reshape(steps, seqs, channels)
    final_ref[:tail] = last_ref[...].astype(jnp.float32)
    final_ref[tail:] = start_ref[...]

    rate = rate_ref[...] * -math.log2(math.e)
    pairs = 2 * states

    def advance(t, carry):
        step_all = step_ref[t]
        xc_all = xc_ref[t].astype(jnp.float32)
        z = z_ref[t].astype(jnp.float32)
        gate = z * jax.nn.sigmoid(z)
        bc = bc_ref[t]
        outputs = []
        for q in range(seqs // 8):
            own = slice(q * 8, q * 8 + 8)
            step, xc = step_all[own], xc_all[own]
            push = step * xc
            output = skip_ref[...] * xc
            for n in range(states):
                b_at, c_at = q * pairs + n, q * pairs + states + n
                state = (
                    jnp.exp2(step * rate[n : n + 1, :]) * final_ref[tail + n, own]
                    + push * bc[:, b_at : b_at + 1]
                )
                final_ref[tail + n, own] = state
                output = output + bc[:, c_at : c_at + 1] * state
            outputs.append(output)
        mixed_ref[t] = (jnp.concatenate(outputs, axis=0) * gate).astype(jnp.bfloat16)
        return carry

    lax.fori_loop(0, steps, advance, 0)


def scan(xz, xc, low, bc, start, dt_weight, dt_bias, decay_rate, skip_gain, tail):
    steps, seqs, channels = xc.shape
    states = decay_rate.shape[0]
    rank = low.shape[2]
    block = min(channels, 512)
    count = channels // block
    return pl.pallas_call(
        scan_kernel,
        grid=(count,),
        out_shape=(
            jax.ShapeDtypeStruct((steps, seqs, channels), jnp.bfloat16),
            jax.ShapeDtypeStruct((tail + states, seqs, channels), jnp.float32),
        ),
        in_specs=[
            pl.BlockSpec((tail, seqs, block), lambda i: (0, 0, i)),
            pl.BlockSpec((steps, seqs, block), lambda i: (0, 0, count + i)),
            pl.BlockSpec((steps, seqs, block), lambda i: (0, 0, i)),
            pl.BlockSpec((steps, seqs, rank), lambda i: (0, 0, 0)),
            pl.BlockSpec(bc.shape, lambda i: (0, 0, 0)),
            pl.BlockSpec((states, seqs, block), lambda i: (0, 0, i)),
            pl.BlockSpec((rank, block), lambda i: (0, i)),
            pl.BlockSpec((1, block), lambda i: (0, i)),
            pl.BlockSpec((states, block), lambda i: (0, i)),
            pl.BlockSpec((1, block), lambda i: (0, i)),
        ],
        out_specs=[
            pl.BlockSpec((steps, seqs, block), lambda i: (0, 0, i)),
            pl.BlockSpec((tail + states, seqs, block), lambda i: (0, 0, i)),
        ],
        scratch_shapes=[pltpu.VMEM((steps, seqs, block), jnp.float32)],
        compiler_params=pltpu.CompilerParams(vmem_limit_bytes=40 * MIB),
    )(
        xz[steps - tail :, :, :channels], xz, xc, low, bc, start, dt_weight,
        dt_bias.reshape(1, channels), decay_rate, skip_gain.reshape(1, channels),
    )


def local(
    groups,
    size,
    in_panels,
    layout,
    hidden,
    prompt_state,
    fork_counts,
    conv_weight,
    conv_bias,
    x_weight,
    dt_weight,
    dt_bias,
    decay_rate,
    skip_gain,
):
    seqs, steps, features = hidden.shape
    panels, panel_rows, _, channels = in_panels.shape
    taps = conv_weight.shape[0]
    rank = dt_weight.shape[0]
    prompts = lax.all_gather(prompt_state, "grp", axis=0, tiled=True)
    weights = in_panels.reshape(panels * panel_rows, 2, channels // 128, 128)
    weights = weights.transpose(0, 2, 1, 3).reshape(-1, 128)
    hid = hidden.reshape(seqs, steps, features // panel_rows, panel_rows).transpose(2, 1, 0, 3)
    own_counts = lax.dynamic_slice_in_dim(fork_counts, lax.axis_index("grp"), 1, 0)
    sources = fork_sources(own_counts, seqs)[0]
    prompt_ids = jnp.arange(prompts.shape[0], dtype=jnp.int32)
    selector = (sources[:, None] == prompt_ids[None, :]).astype(jnp.float32)
    start = jnp.einsum("sp,pkc->ksc", selector, prompts, precision=lax.Precision.HIGHEST)
    xz = project(layout, hid, weights, groups, size)
    xc, low, bc = mix(xz, start[: taps - 1], conv_weight, conv_bias, x_weight, rank, size)
    mixed, final = scan(
        xz, xc, low, bc, start[taps - 1 :], dt_weight, dt_bias, decay_rate, skip_gain, taps - 1
    )
    return mixed.transpose(1, 0, 2), final.transpose(1, 0, 2)


def solution(mesh):
    return jax.shard_map(
        functools.partial(local, mesh.shape["grp"], mesh.shape["tp"]),
        mesh=mesh,
        in_specs=(
            P("grp", None, None, "tp"),
            P(),
            P("grp", None, "tp"),
            P("grp", None, "tp"),
            P(),
            P(None, "tp"),
            P("tp"),
            P("tp", None),
            P(None, "tp"),
            P("tp"),
            P(None, "tp"),
            P("tp"),
        ),
        out_specs=(P("grp", None, "tp"), P("grp", None, "tp")),
        check_vma=False,
    )
```
